256 devices in a mesh: crow: 16 (over y, x), ccol: 8 (over z), lvl: 2 (over core).
Axes of the slice: x: 4, y: 4, z: 8, core: 2. Of those that a mesh axis runs over, the one named last changes fastest.
Arguments:
- x_field: bfloat16 [16, 16, 2, 8, 256], P('crow', 'ccol', 'lvl'), may hold values from -6 to 6
- near_blocks: bfloat16 [16, 8, 2, 64, 256, 256], P('crow', 'ccol', 'lvl'), may hold values from -0.0625 to 0.0625
- near_pairs: int32 [16, 8, 2, 64, 2], P('crow', 'ccol', 'lvl'), may hold values from 0 to 63, as said below
- far_left: bfloat16 [16, 8, 2, 128, 32, 256], P('crow', 'ccol', 'lvl'), may hold values from -0.25 to 0.25
- far_right: bfloat16 [16, 8, 2, 128, 32, 256], P('crow', 'ccol', 'lvl'), may hold values from -0.25 to 0.25
- far_pairs: int32 [16, 8, 2, 128, 2], P('crow', 'ccol', 'lvl'), may hold values from 0 to 63, as said below
- tile_counts: int32 [16, 8, 2, 2], P('crow', 'ccol', 'lvl'), may hold values from 1 to 32, as said below
Outputs:
- product: float32 [16, 16, 2, 8, 256], P('crow', 'ccol', 'lvl')
The draws below stay inside these ranges and needn't reach their ends.
Inputs may be any that keep to these rules, and one draw needn't show every extreme that they name: `near_pairs`: entry 0 is a row-set index below 32, entry 1 a column-set index below 64. `far_pairs`: entry 0 is a row-set index below 32, entry 1 a column-set index below 64. `tile_counts`: entry 0 is at most 16, entry 1 at most 32; some device has all its near slots live and some device all its far slots.
All inputs are finite; a program needn't handle non-finite values.
Results may differ from the reference program's by a relative error of at most 0.0024.
Values may be sent and summed in bfloat16 or wider, within the bound.
A program may use at most 64 MiB of HBM per device.

```python
import jax
import jax.numpy as jnp
from jax import lax

BS = 256
RANK = 32
RHS = 8
TILE = 4
CB = 2
NEAR_DEV = 64
FAR_DEV = 128
NJ = 16
RSET = 32
CSET = 64
N_CROW = 16
N_CCOL = 8
N_LVL = 2


def pair_table(key, slots):
    row_key, col_key = jax.random.split(key)
    shape = (N_CROW, N_CCOL, N_LVL, slots)
    rows = jax.random.randint(row_key, shape, 0, RSET)
    cols = jax.random.randint(col_key, shape, 0, CSET)
    return jnp.stack([rows, cols], axis=-1).astype(jnp.int32)


def draw_near_pairs(key, part):
    key = jax.random.fold_in(key, 11)
    return pair_table(key, NEAR_DEV)


def draw_far_pairs(key, part):
    key = jax.random.fold_in(key, 23)
    return pair_table(key, FAR_DEV)


def draw_tile_counts(key, part):
    key = jax.random.fold_in(key, 37)
    keys = jax.random.split(key, 6)
    near_full = NEAR_DEV // TILE
    far_full = FAR_DEV // TILE
    shape = (N_CROW, N_CCOL)
    heavy_near = jax.random.randint(keys[0], shape, near_full // 2, near_full + 1)
    light_near = jax.random.randint(keys[1], shape, 1, max(1, near_full // 4) + 1)
    heavy_far = jax.random.randint(keys[2], shape, far_full // 2, far_full + 1)
    light_far = jax.random.randint(keys[3], shape, 1, max(1, far_full // 4) + 1)
    places = jnp.arange(N_CROW * N_CCOL, dtype=jnp.int32).reshape(shape)
    near_pick = jax.random.randint(keys[4], (), 0, N_CROW * N_CCOL)
    far_pick = jax.random.randint(keys[5], (), 0, N_CROW * N_CCOL)
    heavy_near = jnp.where(places == near_pick, near_full, heavy_near)
    heavy_far = jnp.where(places == far_pick, far_full, heavy_far)
    near = jnp.stack([heavy_near, light_near], axis=2)
    far = jnp.stack([light_far, heavy_far], axis=2)
    return jnp.stack([near, far], axis=3).astype(jnp.int32)


def steps_of(own_key, dims, shards, smallest, top_value):
    loudness, own = 1.0, jax.random.fold_in(own_key, 6)
    for dim, parts in shards:
        steps = jnp.exp(jax.random.uniform(jax.random.fold_in(own, dim), (parts,), jnp.float32, smallest / len(shards), top_value / len(shards)))
        loudness = loudness * jnp.repeat(steps, dims[dim] // parts).reshape([-1 if axis == dim else 1 for axis in range(len(dims))])
    return loudness


def gaussian(rng, dims, width, limit, pieces=(), held_as=jnp.bfloat16):
    loudness = steps_of(rng, dims, pieces, -0.22, 0.18) if pieces else 1.0
    entries = jax.random.normal(rng, dims, jnp.float32) * width * loudness
    return jnp.minimum(jnp.maximum(entries, -limit), limit).astype(held_as)


def setup_inputs(seed: int = 0) -> dict:
    key_of = jax.random.split(jax.random.key(seed), 8)
    return {
        "x_field": gaussian(key_of[0], (N_CROW, NJ, N_LVL, RHS, BS), 1.0, 6.0, ((0, 16), (1, 8), (2, 2))),
        "near_blocks": gaussian(key_of[1], (N_CROW, N_CCOL, N_LVL, NEAR_DEV, BS, BS), (32 * BS) ** -0.5, 0.0625, ((0, 16), (1, 8), (2, 2))),
        "near_pairs": draw_near_pairs(jax.random.fold_in(key_of[7], 71), 0),
        "far_left": gaussian(key_of[3], (N_CROW, N_CCOL, N_LVL, FAR_DEV, RANK, BS), (2 * BS) ** -0.5, 0.25, ((0, 16), (1, 8), (2, 2))),
        "far_right": gaussian(key_of[4], (N_CROW, N_CCOL, N_LVL, FAR_DEV, RANK, BS), (2 * BS) ** -0.5, 0.25, ((0, 16), (1, 8), (2, 2))),
        "far_pairs": draw_far_pairs(jax.random.fold_in(key_of[7], 71), 0),
        "tile_counts": draw_tile_counts(jax.random.fold_in(key_of[7], 71), 0),
    }


def rounded(value):
    return lax.optimization_barrier(value.astype(jnp.bfloat16)).astype(jnp.float32)


def reference(x_field, near_blocks, near_pairs, far_left, far_right, far_pairs, tile_counts):
    holders = N_CROW * N_CCOL * N_LVL
    total = N_CROW * NJ * N_LVL
    flat = x_field.reshape(total, RHS, BS)
    holder_ids = jnp.arange(holders, dtype=jnp.int32)
    row_block = (holder_ids // (N_CCOL * N_LVL)).astype(jnp.int32)
    col_block = ((holder_ids // N_LVL) % N_CCOL).astype(jnp.int32)
    inputs = (near_blocks.reshape(holders, NEAR_DEV, BS, BS), near_pairs.reshape(holders, NEAR_DEV, 2),
              far_left.reshape(holders, FAR_DEV, RANK, BS), far_right.reshape(holders, FAR_DEV, RANK, BS),
              far_pairs.reshape(holders, FAR_DEV, 2), tile_counts.reshape(holders, 2), row_block, col_block)

    def column_global(index, block):
        upper = index // (CB * N_LVL)
        middle = (index // N_LVL) % CB
        lower = index % N_LVL
        return ((upper * NJ + block * CB + middle) * N_LVL + lower).astype(jnp.int32)

    def step(accum, item):
        blocks, npairs, left, right, fpairs, counts, rblock, cblock = item
        near_live = (jnp.arange(NEAR_DEV, dtype=jnp.int32) < counts[0] * TILE).astype(jnp.float32)[:, None, None]
        rows = (rblock * RSET + npairs[:, 0]).astype(jnp.int32)
        cols = column_global(npairs[:, 1], cblock)
        dense = blocks.astype(jnp.float32)
        forward = jnp.einsum('pab,psb->psa', dense, flat[cols].astype(jnp.float32)) * near_live
        backward = jnp.einsum('pab,psa->psb', dense, flat[rows].astype(jnp.float32)) * near_live
        accum = accum.at[rows].add(forward).at[cols].add(backward)
        far_live = (jnp.arange(FAR_DEV, dtype=jnp.int32) < counts[1] * TILE).astype(jnp.float32)[:, None, None]
        frows = (rblock * RSET + fpairs[:, 0]).astype(jnp.int32)
        fcols = column_global(fpairs[:, 1], cblock)
        left32 = left.astype(jnp.float32)
        right32 = right.astype(jnp.float32)
        coef_col = rounded(jnp.einsum('pkb,psb->psk', right32, flat[fcols].astype(jnp.float32)))
        coef_row = rounded(jnp.einsum('pka,psa->psk', left32, flat[frows].astype(jnp.float32)))
        far_forward = jnp.einsum('pka,psk->psa', left32, coef_col) * far_live
        far_backward = jnp.einsum('pkb,psk->psb', right32, coef_row) * far_live
        accum = accum.at[frows].add(far_forward).at[fcols].add(far_backward)
        return accum, None

    accum, _ = lax.scan(step, jnp.zeros((total, RHS, BS), jnp.float32), inputs)
    return accum.reshape(N_CROW, NJ, N_LVL, RHS, BS)
```

```python
import functools

import jax
import jax.numpy as jnp
from jax import lax
from jax.experimental import pallas as pl
from jax.experimental.pallas import tpu as pltpu
from jax.sharding import PartitionSpec as P

TILE = 4
GROUP = 8
F32 = jnp.float32
BF16 = jnp.bfloat16
NT = (((1,), (1,)), ((), ()))
MESH = pl.DeviceIdType.MESH


def swap_low(value):
    return (value & -4) | ((value & 1) << 1) | ((value >> 1) & 1)


def placement(pairs, count, sets, rhs):
    slots = pairs.shape[1]
    live = lax.broadcasted_iota(jnp.int32, (1, slots), 1) < count * TILE
    wide = slots * rhs
    spread = (
        lax.broadcasted_iota(jnp.int32, (slots, wide), 1) // rhs
        == lax.broadcasted_iota(jnp.int32, (slots, wide), 0)
    )
    spread = jnp.where(spread, 1.0, 0.0).astype(BF16)
    inner = lax.broadcasted_iota(jnp.int32, (1, wide), 1) % rhs
    out = []
    for which, total in enumerate(sets):
        index = swap_low(pairs[which : which + 1, :])
        index = jnp.where(live, index, -1).astype(F32).astype(BF16)
        index = jnp.broadcast_to(index, (8, slots))
        target = jnp.dot(index, spread, preferred_element_type=F32)[:1]
        target = target.astype(jnp.int32) * rhs + inner
        rows = lax.broadcasted_iota(jnp.int32, (total * rhs, wide), 0)
        out.append(jnp.where(rows == target, 1.0, 0.0).astype(BF16))
    return out


def kernel(
    n_row, n_col, n_lvl,
    x_hbm, near_hbm, left_hbm, right_hbm, np_hbm, fp_hbm, cnt_hbm,
    out_ref,
    x_ref, np_s, fp_s, cnt_s, np_v, fp_v,
    near, left, right, row_in, col_in, row_x, col_x, row_f, col_f,
    near_kr, near_kc, far_kr, far_kc,
    row_out, col_out, row_back, col_back,
    small_sem, block_sem, near_sem, gsend, grow, gcol, rsend, rrow, rcol,
):
    r, c, k = lax.axis_index("crow"), lax.axis_index("ccol"), lax.axis_index("lvl")
    rhs, width = 8, x_ref.shape[1]
    n_near, n_groups = near.shape[0], left.shape[0]
    near_step = n_near // near_sem.shape[0]
    rp, cp = n_col * n_lvl, n_row * n_lvl
    me_r, me_c = c * n_lvl + k, r * n_lvl + k

    small = [
        pltpu.make_async_copy(src, dst, small_sem.at[i])
        for i, (src, dst) in enumerate(
            ((x_hbm, x_ref), (np_hbm, np_v), (fp_hbm, fp_v), (cnt_hbm, cnt_s), (np_hbm, np_s), (fp_hbm, fp_s))
        )
    ]
    for copy in small:
        copy.start()
    far_copies = [
        pltpu.make_async_copy(left_hbm, left, block_sem.at[0]),
        pltpu.make_async_copy(right_hbm, right, block_sem.at[1]),
    ]
    for copy in far_copies:
        copy.start()

    def near_copy(step):
        part = pl.ds(step * near_step, near_step)
        return pltpu.make_async_copy(near_hbm.at[part], near.at[part], near_sem.at[step])

    for step in range(near_sem.shape[0]):
        near_copy(step).start()

    barrier = pltpu.get_barrier_semaphore()

    def row_peer(o):
        to = lax.rem(me_r + o, rp)
        return to, {"crow": r, "ccol": to // n_lvl, "lvl": lax.rem(to, n_lvl)}

    def col_peer(o):
        to = lax.rem(me_c + o, cp)
        return to, {"crow": to // n_lvl, "ccol": c, "lvl": lax.rem(to, n_lvl)}

    def greet(peer):
        def body(o, carry):
            pl.semaphore_signal(barrier, inc=1, device_id=peer(o)[1], device_id_type=MESH)
            return carry

        return body

    lax.fori_loop(1, rp, greet(row_peer), 0)
    lax.fori_loop(1, cp, greet(col_peer), 0)

    for copy in small:
        copy.wait()
    row_in[me_r] = x_ref[...]
    col_in[me_c] = x_ref[...]
    near_kr[...], near_kc[...] = placement(np_v[...], cnt_s[0], (2 * rp, 2 * cp), rhs)
    far_kr[...], far_kc[...] = placement(fp_v[...], cnt_s[1], (2 * rp, 2 * cp), rhs)

    pl.semaphore_wait(barrier, rp - 1 + cp - 1)

    def send_x(peer, buf, mine, sem):
        def body(o, carry):
            pltpu.make_async_remote_copy(
                src_ref=x_ref, dst_ref=buf.at[mine], send_sem=gsend, recv_sem=sem,
                device_id=peer(o)[1], device_id_type=MESH,
            ).start()
            return carry

        return body

    lax.fori_loop(1, rp, send_x(row_peer, row_in, me_r, grow), 0)
    lax.fori_loop(1, cp, send_x(col_peer, col_in, me_c, gcol), 0)

    def drain(buf, count, sem):
        part = buf.at[pl.ds(0, count)]
        pltpu.make_async_copy(part, part, sem).wait()

    drain(row_in, rp - 1, grow)
    drain(col_in, cp - 1, gcol)

    def unpack(src, dst):
        def body(a, carry):
            for kk in range(n_lvl):
                v = src[a * n_lvl + kk].astype(F32).reshape(2, rhs, width)
                for jj in range(2):
                    dst[a * 2 * n_lvl + jj * n_lvl + kk] = v[jj]
            return carry

        lax.fori_loop(0, src.shape[0] // n_lvl, body, 0)

    unpack(row_in, row_x)
    unpack(col_in, col_x)

    def near_body(step, carry):
        near_copy(step).wait()
        for u in range(near_step):
            slot = step * near_step + u
            block = near[slot]
            xp = row_x[np_s[0, slot]].astype(BF16)
            xq = col_x[np_s[1, slot]].astype(BF16)
            at = pl.ds(pl.multiple_of(slot * rhs, rhs), rhs)
            row_f[at] = lax.dot_general(xq, block, NT, preferred_element_type=F32)
            col_f[at] = jnp.dot(xp, block, preferred_element_type=F32)
        return carry

    lax.fori_loop(0, near_sem.shape[0], near_body, 0)

    for copy in far_copies:
        copy.wait()
    rank = width // GROUP
    diag = (
        lax.broadcasted_iota(jnp.int32, (GROUP * rhs, width), 0) // rhs
        == lax.broadcasted_iota(jnp.int32, (GROUP * rhs, width), 1) // rank
    )

    def far_body(g, carry):
        xp = jnp.concatenate([row_x[fp_s[0, g * GROUP + u]] for u in range(GROUP)], 0).astype(BF16)
        xq = jnp.concatenate([col_x[fp_s[1, g * GROUP + u]] for u in range(GROUP)], 0).astype(BF16)
        lg, rg = left[g], right[g]
        cq = lax.dot_general(xq, rg, NT, preferred_element_type=F32)
        cr = lax.dot_general(xp, lg, NT, preferred_element_type=F32)
        cq = jnp.where(diag, cq, 0.0).astype(BF16)
        cr = jnp.where(diag, cr, 0.0).astype(BF16)
        at = pl.ds(pl.multiple_of((n_near + g * GROUP) * rhs, GROUP * rhs), GROUP * rhs)
        row_f[at] = jnp.dot(cq, lg, preferred_element_type=F32)
        col_f[at] = jnp.dot(cr, rg, preferred_element_type=F32)
        return carry

    lax.fori_loop(0, n_groups, far_body, 0)

    def scatter(f, kn, kf, out):
        split = n_near * rhs

        def halves(part):
            v = f[part]
            hi = v.astype(BF16)
            return hi, (v - hi.astype(F32)).astype(BF16)

        total = None
        for kmat, part in ((kn, pl.ds(0, split)), (kf, pl.ds(split, f.shape[0] - split))):
            for half in halves(part):
                term = jnp.dot(kmat[...], half, preferred_element_type=F32)
                total = term if total is None else total + term
        out[...] = total.astype(BF16).reshape(out.shape)

    scatter(row_f, near_kr, far_kr, row_out)

    def send_back(peer, src, dst, mine, sem):
        def body(o, carry):
            to, where = peer(o)
            pltpu.make_async_remote_copy(
                src_ref=src.at[to], dst_ref=dst.at[mine], send_sem=rsend, recv_sem=sem,
                device_id=where, device_id_type=MESH,
            ).start()
            return carry

        return body

    lax.fori_loop(1, rp, send_back(row_peer, row_out, row_back, me_r, rrow), 0)
    scatter(col_f, near_kc, far_kc, col_out)
    lax.fori_loop(1, cp, send_back(col_peer, col_out, col_back, me_c, rcol), 0)

    row_back[me_r] = row_out[me_r]
    col_back[me_c] = col_out[me_c]
    drain(row_back, rp - 1, rrow)
    total = row_back[0].astype(F32)
    for a in range(1, rp):
        total = total + row_back[a].astype(F32)
    drain(col_back, cp - 1, rcol)
    for a in range(cp):
        total = total + col_back[a].astype(F32)
    out_ref[...] = total
    drain(row_in, rp - 1, gsend)
    drain(col_in, cp - 1, gsend)
    drain(row_back, rp - 1, rsend)
    drain(col_back, cp - 1, rsend)


def per_device(x_field, near_blocks, near_pairs, far_left, far_right, far_pairs, tile_counts):
    n_row, n_col, n_lvl = (lax.axis_size(a) for a in ("crow", "ccol", "lvl"))
    per, rhs, width = x_field.shape[1], x_field.shape[3], x_field.shape[4]
    n_near, n_far, rank = near_blocks.shape[3], far_left.shape[3], far_left.shape[4]
    n_groups = n_far // GROUP
    x = x_field.reshape(per * rhs, width)
    near = near_blocks.reshape(n_near, width, width)
    left = far_left.reshape(n_groups, GROUP * rank, width)
    right = far_right.reshape(n_groups, GROUP * rank, width)
    npairs = near_pairs.reshape(n_near, 2).T
    fpairs = far_pairs.reshape(n_far, 2).T
    counts = tile_counts.reshape(2)
    rp, cp = n_col * n_lvl, n_row * n_lvl
    rows, cols = per * rp, per * cp
    slots = n_near + n_far
    vmem = pl.BlockSpec(memory_space=pltpu.VMEM)
    hbm = pl.BlockSpec(memory_space=pltpu.HBM)
    dma = pltpu.SemaphoreType.DMA
    out = pl.pallas_call(
        functools.partial(kernel, n_row, n_col, n_lvl),
        out_shape=jax.ShapeDtypeStruct((per * rhs, width), F32),
        in_specs=[hbm] * 7,
        out_specs=vmem,
        scratch_shapes=[
            pltpu.VMEM(x.shape, BF16),
            pltpu.SMEM(npairs.shape, jnp.int32),
            pltpu.SMEM(fpairs.shape, jnp.int32),
            pltpu.SMEM(counts.shape, jnp.int32),
            pltpu.VMEM(npairs.shape, jnp.int32),
            pltpu.VMEM(fpairs.shape, jnp.int32),
            pltpu.VMEM(near.shape, BF16),
            pltpu.VMEM(left.shape, BF16),
            pltpu.VMEM(right.shape, BF16),
            pltpu.VMEM((rp, per * rhs, width), BF16),
            pltpu.VMEM((cp, per * rhs, width), BF16),
            pltpu.VMEM((rows, rhs, width), F32),
            pltpu.VMEM((cols, rhs, width), F32),
            pltpu.VMEM((slots * rhs, width), F32),
            pltpu.VMEM((slots * rhs, width), F32),
            pltpu.VMEM((rows * rhs, n_near * rhs), BF16),
            pltpu.VMEM((cols * rhs, n_near * rhs), BF16),
            pltpu.VMEM((rows * rhs, n_far * rhs), BF16),
            pltpu.VMEM((cols * rhs, n_far * rhs), BF16),
            pltpu.VMEM((rp, per * rhs, width), BF16),
            pltpu.VMEM((cp, per * rhs, width), BF16),
            pltpu.VMEM((rp, per * rhs, width), BF16),
            pltpu.VMEM((cp, per * rhs, width), BF16),
            dma((6,)),
            dma((2,)),
            dma((8,)),
            dma, dma, dma, dma, dma, dma,
        ],
        compiler_params=pltpu.CompilerParams(
            collective_id=0, has_side_effects=True, vmem_limit_bytes=56 * 1024 * 1024
        ),
        cost_estimate=pl.CostEstimate(
            flops=4 * slots * rhs * width * width,
            bytes_accessed=2 * (near.size + left.size + right.size),
            transcendentals=0,
        ),
    )(x, near, left, right, npairs, fpairs, counts)
    return out.reshape(x_field.shape)


def solution(mesh):
    placed = (
        P("crow", "ccol", "lvl", None, None),
        P("crow", "ccol", "lvl", None, None, None),
        P("crow", "ccol", "lvl", None, None),
        P("crow", "ccol", "lvl", None, None, None),
        P("crow", "ccol", "lvl", None, None, None),
        P("crow", "ccol", "lvl", None, None),
        P("crow", "ccol", "lvl", None),
    )
    return jax.shard_map(
        per_device,
        mesh=mesh,
        in_specs=placed,
        out_specs=P("crow", "ccol", "lvl", None, None),
        check_vma=False,
    )
```

```python
import functools

import jax
import jax.numpy as jnp
from jax import lax
from jax.experimental import pallas as pl
from jax.experimental.pallas import tpu as pltpu
from jax.sharding import PartitionSpec as P

TILE = 4
GROUP = 8
UNROLL = 32
F32 = jnp.float32
BF16 = jnp.bfloat16
MESH = pl.DeviceIdType.MESH


def far_first(n):
    return sorted(range(n), key=lambda o: -min(o, n - o))


def chain_tables(pairs, count, which):
    slots = pairs.shape[1]
    by_lane = jnp.broadcast_to(pairs[which : which + 1, :], (slots, slots)).astype(F32)
    by_row = by_lane.T
    t = lax.broadcasted_iota(jnp.int32, (slots, slots), 0)
    s = lax.broadcasted_iota(jnp.int32, (slots, slots), 1)
    before = (by_row == by_lane) & (t < s)
    prev = jnp.max(jnp.where(before, t + 1, 0), axis=0, keepdims=True)
    mine = (by_row == s.astype(F32)) & (t < count * TILE)
    last = jnp.max(jnp.where(mine, t + 1, 0), axis=0, keepdims=True)
    return prev, last


def kernel(
    n_row, n_col, n_lvl,
    x_hbm, near_hbm, left_hbm, right_hbm, np_hbm, fp_hbm, cnt_hbm,
    out_ref,
    x_ref, np_s, fp_s, cnt_s, np_v, fp_v, tab_v, tab_s,
    near, left, right, near_t, left_t, right_t,
    row_in, col_in, row_x, col_x, row_n, row_f, col_n, col_f,
    row_out, col_out, row_back, col_back,
    small_sem, far_sem, near_sem, tab_sem, gsend, grow, gcol, rsend, rrow, rcol,
):
    r, c, k = lax.axis_index("crow"), lax.axis_index("ccol"), lax.axis_index("lvl")
    rhs, width = 8, x_ref.shape[1]
    n_near, n_groups = near.shape[0], left.shape[0]
    n_far = n_groups * GROUP
    rank = width // GROUP
    near_step = n_near // near_sem.shape[0]
    rp, cp = n_col * n_lvl, n_row * n_lvl
    me_r, me_c = c * n_lvl + k, r * n_lvl + k

    nx = 4 if n_row % 4 == 0 else n_row
    ny = n_row // nx
    y, x = r // nx, lax.rem(r, nx)
    zs = [c] + [lax.rem(c + o, n_col) for o in range(1, n_col)]
    ys = [y] + [lax.rem(y + o, ny) for o in range(1, ny)]
    xs = [x] + [lax.rem(x + o, nx) for o in range(1, nx)]
    ks = [k] + [lax.rem(k + o, n_lvl) for o in range(1, n_lvl)]
    row_peers, col_peers = [], []
    for oz in far_first(n_col):
        for ok in range(n_lvl):
            if oz or ok:
                row_peers.append((zs[oz] * n_lvl + ks[ok], {"crow": r, "ccol": zs[oz], "lvl": ks[ok]}))
    grid = [(oy, ox) for oy in range(ny) for ox in range(nx)]
    grid.sort(key=lambda o: -min(o[0], ny - o[0]) - min(o[1], nx - o[1]))
    for oy, ox in grid:
        to = ys[oy] * nx + xs[ox]
        for ok in range(n_lvl):
            if oy or ox or ok:
                col_peers.append((to * n_lvl + ks[ok], {"crow": to, "ccol": c, "lvl": ks[ok]}))

    barrier = pltpu.get_barrier_semaphore()
    for _, where in row_peers + col_peers:
        pl.semaphore_signal(barrier, inc=1, device_id=where, device_id_type=MESH)

    small = [
        pltpu.make_async_copy(src, dst, small_sem.at[i])
        for i, (src, dst) in enumerate(
            ((x_hbm, x_ref), (np_hbm, np_v), (fp_hbm, fp_v), (cnt_hbm, cnt_s), (np_hbm, np_s), (fp_hbm, fp_s))
        )
    ]
    for copy in small:
        copy.start()
    far_copies = [
        pltpu.make_async_copy(left_hbm, left, far_sem.at[0]),
        pltpu.make_async_copy(right_hbm, right, far_sem.at[1]),
    ]

    def near_copy(step):
        part = pl.ds(step * near_step, near_step)
        return pltpu.make_async_copy(near_hbm.at[part], near.at[part], near_sem.at[step])

    for copy in far_copies:
        copy.start()
    for step in range(near_sem.shape[0]):
        near_copy(step).start()

    small[0].wait()
    pl.semaphore_wait(barrier, rp - 1 + cp - 1)
    for peers, buf, mine, sem in ((row_peers, row_in, me_r, grow), (col_peers, col_in, me_c, gcol)):
        for _, where in peers:
            pltpu.make_async_remote_copy(
                src_ref=x_ref, dst_ref=buf.at[mine], send_sem=gsend, recv_sem=sem,
                device_id=where, device_id_type=MESH,
            ).start()

    row_in[me_r] = x_ref[...]
    col_in[me_c] = x_ref[...]
    for copy in small[1:]:
        copy.wait()
    tab_v[...] = jnp.zeros_like(tab_v)
    zero = jnp.zeros((rhs, width), F32)
    for total in (row_n, row_f, col_n, col_f):
        total[0] = zero
    for pairs, count, at in ((np_v, 0, 0), (fp_v, 1, 2)):
        slots = pairs.shape[1]
        for which in range(2):
            prev, last = chain_tables(pairs[...], cnt_s[count], which)
            tab_v[at + which : at + which + 1, :slots] = prev
            tab_v[4 + at + which : 5 + at + which, :slots] = last
    tab_copy = pltpu.make_async_copy(tab_v, tab_s, tab_sem)
    tab_copy.start()

    for copy in far_copies:
        copy.wait()

    def far_turn(g, carry):
        left_t[g] = left[g].T
        right_t[g] = right[g].T
        return carry

    lax.fori_loop(0, n_groups, far_turn, 0)

    def near_turn(step, carry):
        near_copy(step).wait()
        for u in range(near_step):
            slot = step * near_step + u
            near_t[slot] = near[slot].T
        return carry

    lax.fori_loop(0, near_sem.shape[0], near_turn, 0)
    tab_copy.wait()

    def drain(buf, count, sem):
        part = buf.at[pl.ds(0, count)]
        pltpu.make_async_copy(part, part, sem).wait()

    def unpack(src, dst):
        def body(a, carry):
            for kk in range(n_lvl):
                v = src[a * n_lvl + kk].astype(F32).reshape(2, rhs, width)
                for jj in range(2):
                    dst[a * 2 * n_lvl + jj * n_lvl + kk] = v[jj]
            return carry

        lax.fori_loop(0, src.shape[0] // n_lvl, body, 0)

    diag = (
        lax.broadcasted_iota(jnp.int32, (GROUP * rhs, width), 0) // rhs
        == lax.broadcasted_iota(jnp.int32, (GROUP * rhs, width), 1) // rank
    )
    far_u = UNROLL * n_groups // n_near

    def one_way(field, side, blocks, first, second, near_sum, far_sum, chain):
        def body(step, carry):
            for u in range(UNROLL):
                slot = step * UNROLL + u
                v = field[np_s[side, slot]].astype(BF16)
                part = jnp.dot(v, blocks[slot], preferred_element_type=F32)
                near_sum[slot + 1] = part + near_sum[tab_s[chain, slot]]
            for u in range(far_u):
                g = step * far_u + u
                v = jnp.concatenate([field[fp_s[side, g * GROUP + w]] for w in range(GROUP)], 0)
                coef = jnp.dot(v.astype(BF16), first[g], preferred_element_type=F32)
                coef = jnp.where(diag, coef, 0.0).astype(BF16)
                part = jnp.dot(coef, second[g], preferred_element_type=F32)
                for w in range(GROUP):
                    slot = g * GROUP + w
                    far_sum[slot + 1] = part[w * rhs : (w + 1) * rhs] + far_sum[tab_s[2 + chain, slot]]
            return carry

        lax.fori_loop(0, n_near // UNROLL, body, 0)

    def collect(near_sum, far_sum, chain, out):
        def body(a, carry):
            for kk in range(n_lvl):
                parts = []
                for jj in range(2):
                    p = a * 2 * n_lvl + jj * n_lvl + kk
                    parts.append(near_sum[tab_s[4 + chain, p]] + far_sum[tab_s[6 + chain, p]])
                out[a * n_lvl + kk] = jnp.concatenate(parts, 0).astype(BF16)
            return carry

        lax.fori_loop(0, out.shape[0] // n_lvl, body, 0)

    def send_back(peers, src, dst, mine, sem):
        for to, where in peers:
            pltpu.make_async_remote_copy(
                src_ref=src.at[to], dst_ref=dst.at[mine], send_sem=rsend, recv_sem=sem,
                device_id=where, device_id_type=MESH,
            ).start()

    drain(row_in, rp - 1, grow)
    unpack(row_in, row_x)
    one_way(row_x, 0, near, left_t, right, col_n, col_f, 1)
    collect(col_n, col_f, 1, col_out)
    send_back(col_peers, col_out, col_back, me_c, rcol)

    drain(col_in, cp - 1, gcol)
    unpack(col_in, col_x)
    one_way(col_x, 1, near_t, right_t, left, row_n, row_f, 0)
    collect(row_n, row_f, 0, row_out)
    send_back(row_peers, row_out, row_back, me_r, rrow)

    col_back[me_c] = col_out[me_c]
    row_back[me_r] = row_out[me_r]
    drain(col_back, cp - 1, rcol)
    total = col_back[0].astype(F32)
    for a in range(1, cp):
        total = total + col_back[a].astype(F32)
    drain(row_back, rp - 1, rrow)
    for a in range(rp):
        total = total + row_back[a].astype(F32)
    out_ref[...] = total
    drain(row_in, rp - 1, gsend)
    drain(col_in, cp - 1, gsend)
    drain(row_back, rp - 1, rsend)
    drain(col_back, cp - 1, rsend)


def per_device(x_field, near_blocks, near_pairs, far_left, far_right, far_pairs, tile_counts):
    n_row, n_col, n_lvl = (lax.axis_size(a) for a in ("crow", "ccol", "lvl"))
    per, rhs, width = x_field.shape[1], x_field.shape[3], x_field.shape[4]
    n_near, n_far, rank = near_blocks.shape[3], far_left.shape[3], far_left.shape[4]
    n_groups = n_far // GROUP
    x = x_field.reshape(per * rhs, width)
    near = near_blocks.reshape(n_near, width, width)
    left = far_left.reshape(n_groups, GROUP * rank, width)
    right = far_right.reshape(n_groups, GROUP * rank, width)
    npairs = near_pairs.reshape(n_near, 2).T
    fpairs = far_pairs.reshape(n_far, 2).T
    counts = tile_counts.reshape(2)
    rp, cp = n_col * n_lvl, n_row * n_lvl
    rows, cols = per * rp, per * cp
    vmem = pl.BlockSpec(memory_space=pltpu.VMEM)
    hbm = pl.BlockSpec(memory_space=pltpu.HBM)
    dma = pltpu.SemaphoreType.DMA
    operands = [
        pltpu.with_memory_space_constraint(a, pltpu.HBM)
        for a in (x, near, left, right, npairs, fpairs, counts)
    ]
    out = pl.pallas_call(
        functools.partial(kernel, n_row, n_col, n_lvl),
        out_shape=jax.ShapeDtypeStruct((per * rhs, width), F32),
        in_specs=[hbm] * 7,
        out_specs=vmem,
        scratch_shapes=[
            pltpu.VMEM(x.shape, BF16),
            pltpu.SMEM(npairs.shape, jnp.int32),
            pltpu.SMEM(fpairs.shape, jnp.int32),
            pltpu.SMEM(counts.shape, jnp.int32),
            pltpu.VMEM(npairs.shape, jnp.int32),
            pltpu.VMEM(fpairs.shape, jnp.int32),
            pltpu.VMEM((8, 128), jnp.int32),
            pltpu.SMEM((8, 128), jnp.int32),
            pltpu.VMEM(near.shape, BF16),
            pltpu.VMEM(left.shape, BF16),
            pltpu.VMEM(right.shape, BF16),
            pltpu.VMEM(near.shape, BF16),
            pltpu.VMEM(left.shape, BF16),
            pltpu.VMEM(right.shape, BF16),
            pltpu.VMEM((rp, per * rhs, width), BF16),
            pltpu.VMEM((cp, per * rhs, width), BF16),
            pltpu.VMEM((rows, rhs, width), F32),
            pltpu.VMEM((cols, rhs, width), F32),
            pltpu.VMEM((n_near + 1, rhs, width), F32),
            pltpu.VMEM((n_far + 1, rhs, width), F32),
            pltpu.VMEM((n_near + 1, rhs, width), F32),
            pltpu.VMEM((n_far + 1, rhs, width), F32),
            pltpu.VMEM((rp, per * rhs, width), BF16),
            pltpu.VMEM((cp, per * rhs, width), BF16),
            pltpu.VMEM((rp, per * rhs, width), BF16),
            pltpu.VMEM((cp, per * rhs, width), BF16),
            dma((6,)),
            dma((2,)),
            dma((8,)),
            dma, dma, dma, dma, dma, dma, dma,
        ],
        compiler_params=pltpu.CompilerParams(
            collective_id=0, has_side_effects=True, vmem_limit_bytes=40 * 1024 * 1024
        ),
        cost_estimate=pl.CostEstimate(
            flops=4 * (n_near + n_far) * rhs * width * width,
            bytes_accessed=2 * (near.size + left.size + right.size),
            transcendentals=0,
        ),
    )(*operands)
    return out.reshape(x_field.shape)


def solution(mesh):
    placed = (
        P("crow", "ccol", "lvl", None, None),
        P("crow", "ccol", "lvl", None, None, None),
        P("crow", "ccol", "lvl", None, None),
        P("crow", "ccol", "lvl", None, None, None),
        P("crow", "ccol", "lvl", None, None, None),
        P("crow", "ccol", "lvl", None, None),
        P("crow", "ccol", "lvl", None),
    )
    return jax.shard_map(
        per_device,
        mesh=mesh,
        in_specs=placed,
        out_specs=P("crow", "ccol", "lvl", None, None),
        check_vma=False,
    )
```

```python
import functools

import jax
import jax.numpy as jnp
from jax import lax
from jax.experimental import pallas as pl
from jax.experimental.pallas import tpu as pltpu
from jax.sharding import PartitionSpec as P

TILE = 4
GROUP = 8
CHUNK = 4
LAG = 1
EARLY = 2
F32 = jnp.float32
BF16 = jnp.bfloat16
MESH = pl.DeviceIdType.MESH


def far_first(n):
    return sorted(range(n), key=lambda o: -min(o, n - o))


def chain_tables(pairs, count, which):
    slots = pairs.shape[1]
    by_lane = jnp.broadcast_to(pairs[which : which + 1, :], (slots, slots)).astype(F32)
    by_row = by_lane.T
    t = lax.broadcasted_iota(jnp.int32, (slots, slots), 0)
    s = lax.broadcasted_iota(jnp.int32, (slots, slots), 1)
    before = (by_row == by_lane) & (t < s)
    prev = jnp.max(jnp.where(before, t + 1, 0), axis=0, keepdims=True)
    mine = (by_row == s.astype(F32)) & (t < count * TILE)
    last = jnp.max(jnp.where(mine, t + 1, 0), axis=0, keepdims=True)
    return prev, last


def kernel(
    n_row, n_col, n_lvl,
    x_hbm, near_hbm, left_hbm, right_hbm, np_hbm, fp_hbm, cnt_hbm,
    out_ref,
    x_ref, np_s, fp_s, cnt_s, np_v, fp_v, tab_v, tab_s,
    near, left, right, near_t, left_t, right_t,
    row_in, col_in, row_x, col_x, row_n, row_f, col_n, col_f,
    row_out, col_out, row_back, col_back,
    small_sem, far_sem, near_sem, tab_sem, gsend, grow, gcol, rsend, rrow, rcol, ready,
):
    r, c, k = lax.axis_index("crow"), lax.axis_index("ccol"), lax.axis_index("lvl")
    rhs, width = 8, x_ref.shape[1]
    n_near, n_groups = near.shape[0], left.shape[0]
    n_far = n_groups * GROUP
    rank = width // GROUP
    near_step = n_near // near_sem.shape[0]
    rp, cp = n_col * n_lvl, n_row * n_lvl
    me_r, me_c = c * n_lvl + k, r * n_lvl + k

    nx = 4 if n_row % 4 == 0 else n_row
    ny = n_row // nx
    y, x = r // nx, lax.rem(r, nx)
    zs = [c] + [lax.rem(c + o, n_col) for o in range(1, n_col)]
    ys = [y] + [lax.rem(y + o, ny) for o in range(1, ny)]
    xs = [x] + [lax.rem(x + o, nx) for o in range(1, nx)]
    ks = [k] + [lax.rem(k + o, n_lvl) for o in range(1, n_lvl)]
    row_peers, col_peers = [], []
    for oz in far_first(n_col):
        for ok in range(n_lvl):
            if oz or ok:
                row_peers.append((zs[oz] * n_lvl + ks[ok], {"crow": r, "ccol": zs[oz], "lvl": ks[ok]}))
    grid = [(oy, ox) for oy in range(ny) for ox in range(nx)]
    grid.sort(key=lambda o: -min(o[0], ny - o[0]) - min(o[1], nx - o[1]))
    for oy, ox in grid:
        to = ys[oy] * nx + xs[ox]
        for ok in range(n_lvl):
            if oy or ox or ok:
                col_peers.append((to * n_lvl + ks[ok], {"crow": to, "ccol": c, "lvl": ks[ok]}))

    barrier = pltpu.get_barrier_semaphore()
    other = {"lvl": 1 - k}
    for ahead, peers in ((0, col_peers), (1, row_peers)):
        for at in range(0, len(peers) - 1, n_lvl):
            where = {**peers[at][1], "lvl": jnp.int32(ahead)}
            pl.semaphore_signal(barrier, inc=1, device_id=where, device_id_type=MESH)

        @pl.when(k != ahead)
        def _():
            pl.semaphore_signal(barrier, inc=1, device_id=other, device_id_type=MESH)

    small = [
        pltpu.make_async_copy(src, dst, small_sem.at[i])
        for i, (src, dst) in enumerate(
            ((x_hbm, x_ref), (np_hbm, np_v), (fp_hbm, fp_v), (cnt_hbm, cnt_s), (np_hbm, np_s), (fp_hbm, fp_s))
        )
    ]
    for copy in small:
        copy.start()
    far_copies = [
        pltpu.make_async_copy(left_hbm, left, far_sem.at[0]),
        pltpu.make_async_copy(right_hbm, right, far_sem.at[1]),
    ]

    def near_copy(step):
        part = pl.ds(step * near_step, near_step)
        return pltpu.make_async_copy(near_hbm.at[part], near.at[part], near_sem.at[step])

    for copy in far_copies:
        copy.start()
    for step in range(near_sem.shape[0]):
        near_copy(step).start()

    small[0].wait()
    def meet_and_send(ahead, peers, buf, mine, sem):
        @pl.when(k == ahead)
        def _():
            pl.semaphore_wait(barrier, len(peers))
            pl.semaphore_signal(ready, inc=1, device_id=other, device_id_type=MESH)

        @pl.when(k != ahead)
        def _():
            pl.semaphore_wait(ready, 1)

        for _, where in peers:
            pltpu.make_async_remote_copy(
                src_ref=x_ref, dst_ref=buf.at[mine], send_sem=gsend, recv_sem=sem,
                device_id=where, device_id_type=MESH,
            ).start()

    meet_cols = functools.partial(meet_and_send, 0, col_peers, col_in, me_c, gcol)
    meet_rows = functools.partial(meet_and_send, 1, row_peers, row_in, me_r, grow)

    @pl.when(c >= EARLY)
    def _():
        meet_rows()
        meet_cols()

    pl.when(c < EARLY)(meet_cols)

    row_in[me_r] = x_ref[...]
    col_in[me_c] = x_ref[...]
    for copy in small[1:]:
        copy.wait()
    tab_v[...] = jnp.zeros_like(tab_v)
    zero = jnp.zeros((rhs, width), F32)
    for total in (row_n, row_f, col_n, col_f):
        total[0] = zero
    for pairs, count, at in ((np_v, 0, 0), (fp_v, 1, 2)):
        slots = pairs.shape[1]
        for which in range(2):
            prev, last = chain_tables(pairs[...], cnt_s[count], which)
            tab_v[at + which : at + which + 1, :slots] = prev
            tab_v[4 + at + which : 5 + at + which, :slots] = last
    tab_copy = pltpu.make_async_copy(tab_v, tab_s, tab_sem)
    tab_copy.start()

    for copy in far_copies:
        copy.wait()

    def far_turn(g, carry):
        left_t[g] = left[g].T
        right_t[g] = right[g].T
        return carry

    lax.fori_loop(0, n_groups, far_turn, 0)

    def near_turn(step, carry):
        near_copy(step).wait()
        for u in range(near_step):
            slot = step * near_step + u
            near_t[slot] = near[slot].T
        return carry

    lax.fori_loop(0, near_sem.shape[0], near_turn, 0)
    tab_copy.wait()
    pl.when(c < EARLY)(meet_rows)

    def drain(buf, count, sem):
        part = buf.at[pl.ds(0, count)]
        pltpu.make_async_copy(part, part, sem).wait()

    def unpack(src, dst):
        def body(a, carry):
            for kk in range(n_lvl):
                v = src[a * n_lvl + kk].astype(F32).reshape(2, rhs, width)
                for jj in range(2):
                    dst[a * 2 * n_lvl + jj * n_lvl + kk] = v[jj]
            return carry

        lax.fori_loop(0, src.shape[0] // n_lvl, body, 0, unroll=4)

    diag = (
        lax.broadcasted_iota(jnp.int32, (GROUP * rhs, width), 0) // rhs
        == lax.broadcasted_iota(jnp.int32, (GROUP * rhs, width), 1) // rank
    )
    def one_way(field, side, blocks, first, second, near_sum, far_sum, chain):
        every = n_near // n_groups

        def coefficients(g):
            v = jnp.concatenate([field[fp_s[side, g * GROUP + w]] for w in range(GROUP)], 0)
            coef = jnp.dot(v.astype(BF16), first[g], preferred_element_type=F32)
            return jnp.where(diag, coef, 0.0).astype(BF16)

        def near_slot(slot):
            v = field[np_s[side, slot]].astype(BF16)
            part = jnp.dot(v, blocks[slot], preferred_element_type=F32)
            near_sum[slot + 1] = part + near_sum[tab_s[chain, slot]]

        def far_group(g, coef):
            part = jnp.dot(coef, second[g], preferred_element_type=F32)
            for w in range(GROUP):
                slot = g * GROUP + w
                far_sum[slot + 1] = part[w * rhs : (w + 1) * rhs] + far_sum[tab_s[2 + chain, slot]]

        coefs = {}
        for g in range(n_groups + LAG):
            if g < n_groups:
                coefs[g] = coefficients(g)
                for slot in range(g * every, (g + 1) * every):
                    near_slot(slot)
            if g >= LAG:
                far_group(g - LAG, coefs.pop(g - LAG))

    def collect(near_sum, far_sum, chain, out, to):
        first = 2 * n_lvl * (to // n_lvl) + lax.rem(to, n_lvl)
        parts = []
        for jj in range(2):
            p = first + jj * n_lvl
            parts.append(near_sum[tab_s[4 + chain, p]] + far_sum[tab_s[6 + chain, p]])
        out[to] = jnp.concatenate(parts, 0).astype(BF16)

    def give_back(src, dst, mine, sem, to, where):
        pltpu.make_async_remote_copy(
            src_ref=src.at[to], dst_ref=dst.at[mine], send_sem=rsend, recv_sem=sem,
            device_id=where, device_id_type=MESH,
        ).start()

    def give_all(near_sum, far_sum, chain, peers, src, dst, mine, sem):
        for at in range(0, len(peers), CHUNK):
            for to, _ in peers[at : at + CHUNK]:
                collect(near_sum, far_sum, chain, src, to)
            for peer in peers[at : at + CHUNK]:
                give_back(src, dst, mine, sem, *peer)
        collect(near_sum, far_sum, chain, dst, mine)

    drain(col_in, cp - 1, gcol)
    unpack(col_in, col_x)
    one_way(col_x, 1, near_t, right_t, left, row_n, row_f, 0)
    give_all(row_n, row_f, 0, row_peers, row_out, row_back, me_r, rrow)

    drain(row_in, rp - 1, grow)
    unpack(row_in, row_x)
    one_way(row_x, 0, near, left_t, right, col_n, col_f, 1)
    give_all(col_n, col_f, 1, col_peers, col_out, col_back, me_c, rcol)

    drain(row_back, rp - 1, rrow)
    total = row_back[0].astype(F32)
    for a in range(1, rp):
        total = total + row_back[a].astype(F32)
    drain(col_back, cp - 1, rcol)
    for a in range(cp):
        total = total + col_back[a].astype(F32)
    out_ref[...] = total
    drain(row_in, rp - 1, gsend)
    drain(col_in, cp - 1, gsend)
    drain(row_back, rp - 1, rsend)
    drain(col_back, cp - 1, rsend)


def per_device(x_field, near_blocks, near_pairs, far_left, far_right, far_pairs, tile_counts):
    n_row, n_col, n_lvl = (lax.axis_size(a) for a in ("crow", "ccol", "lvl"))
    per, rhs, width = x_field.shape[1], x_field.shape[3], x_field.shape[4]
    n_near, n_far, rank = near_blocks.shape[3], far_left.shape[3], far_left.shape[4]
    n_groups = n_far // GROUP
    x = x_field.reshape(per * rhs, width)
    near = near_blocks.reshape(n_near, width, width)
    left = far_left.reshape(n_groups, GROUP * rank, width)
    right = far_right.reshape(n_groups, GROUP * rank, width)
    npairs = near_pairs.reshape(n_near, 2).T
    fpairs = far_pairs.reshape(n_far, 2).T
    counts = tile_counts.reshape(2)
    rp, cp = n_col * n_lvl, n_row * n_lvl
    rows, cols = per * rp, per * cp
    vmem = pl.BlockSpec(memory_space=pltpu.VMEM)
    hbm = pl.BlockSpec(memory_space=pltpu.HBM)
    dma = pltpu.SemaphoreType.DMA
    operands = [
        pltpu.with_memory_space_constraint(a, pltpu.HBM)
        for a in (x, near, left, right, npairs, fpairs, counts)
    ]
    out = pl.pallas_call(
        functools.partial(kernel, n_row, n_col, n_lvl),
        out_shape=jax.ShapeDtypeStruct((per * rhs, width), F32),
        in_specs=[hbm] * 7,
        out_specs=vmem,
        scratch_shapes=[
            pltpu.VMEM(x.shape, BF16),
            pltpu.SMEM(npairs.shape, jnp.int32),
            pltpu.SMEM(fpairs.shape, jnp.int32),
            pltpu.SMEM(counts.shape, jnp.int32),
            pltpu.VMEM(npairs.shape, jnp.int32),
            pltpu.VMEM(fpairs.shape, jnp.int32),
            pltpu.VMEM((8, 128), jnp.int32),
            pltpu.SMEM((8, 128), jnp.int32),
            pltpu.VMEM(near.shape, BF16),
            pltpu.VMEM(left.shape, BF16),
            pltpu.VMEM(right.shape, BF16),
            pltpu.VMEM(near.shape, BF16),
            pltpu.VMEM(left.shape, BF16),
            pltpu.VMEM(right.shape, BF16),
            pltpu.VMEM((rp, per * rhs, width), BF16),
            pltpu.VMEM((cp, per * rhs, width), BF16),
            pltpu.VMEM((rows, rhs, width), F32),
            pltpu.VMEM((cols, rhs, width), F32),
            pltpu.VMEM((n_near + 1, rhs, width), F32),
            pltpu.VMEM((n_far + 1, rhs, width), F32),
            pltpu.VMEM((n_near + 1, rhs, width), F32),
            pltpu.VMEM((n_far + 1, rhs, width), F32),
            pltpu.VMEM((rp, per * rhs, width), BF16),
            pltpu.VMEM((cp, per * rhs, width), BF16),
            pltpu.VMEM((rp, per * rhs, width), BF16),
            pltpu.VMEM((cp, per * rhs, width), BF16),
            dma((6,)),
            dma((2,)),
            dma((8,)),
            dma, dma, dma, dma, dma, dma, dma,
            pltpu.SemaphoreType.REGULAR,
        ],
        compiler_params=pltpu.CompilerParams(
            collective_id=0, has_side_effects=True, vmem_limit_bytes=40 * 1024 * 1024
        ),
        cost_estimate=pl.CostEstimate(
            flops=4 * (n_near + n_far) * rhs * width * width,
            bytes_accessed=2 * (near.size + left.size + right.size),
            transcendentals=0,
        ),
    )(*operands)
    return out.reshape(x_field.shape)


def solution(mesh):
    placed = (
        P("crow", "ccol", "lvl", None, None),
        P("crow", "ccol", "lvl", None, None, None),
        P("crow", "ccol", "lvl", None, None),
        P("crow", "ccol", "lvl", None, None, None),
        P("crow", "ccol", "lvl", None, None, None),
        P("crow", "ccol", "lvl", None, None),
        P("crow", "ccol", "lvl", None),
    )
    return jax.shard_map(
        per_device,
        mesh=mesh,
        in_specs=placed,
        out_specs=P("crow", "ccol", "lvl", None, None),
        check_vma=False,
    )
```

```python
import functools

import jax
import jax.numpy as jnp
from jax import lax
from jax.experimental import pallas as pl
from jax.experimental.pallas import tpu as pltpu
from jax.sharding import PartitionSpec as P

TILE = 4
GROUP = 8
CHUNK = 4
LAG = 1
STAGES = (3, 2, 1, 0)
F32 = jnp.float32
BF16 = jnp.bfloat16
MESH = pl.DeviceIdType.MESH


def far_first(n):
    return sorted(range(n), key=lambda o: -min(o, n - o))


def chain_tables(pairs, count, which):
    slots = pairs.shape[1]
    by_lane = jnp.broadcast_to(pairs[which : which + 1, :], (slots, slots)).astype(F32)
    by_row = by_lane.T
    t = lax.broadcasted_iota(jnp.int32, (slots, slots), 0)
    s = lax.broadcasted_iota(jnp.int32, (slots, slots), 1)
    before = (by_row == by_lane) & (t < s)
    prev = jnp.max(jnp.where(before, t + 1, 0), axis=0, keepdims=True)
    mine = (by_row == s.astype(F32)) & (t < count * TILE)
    last = jnp.max(jnp.where(mine, t + 1, 0), axis=0, keepdims=True)
    return prev, last


def kernel(
    n_row, n_col, n_lvl,
    x_hbm, near_hbm, left_hbm, right_hbm, np_hbm, fp_hbm, cnt_hbm,
    out_ref,
    x_ref, np_s, fp_s, cnt_s, np_v, fp_v, tab_v, tab_s,
    near, left, right, near_t, left_t, right_t,
    row_in, col_in, row_x, col_x, row_n, row_f, col_n, col_f,
    row_out, col_out, row_back, col_back,
    small_sem, far_sem, near_sem, tab_sem, gsend, grow, gcol, rsend, rrow, rcol, ready,
):
    r, c, k = lax.axis_index("crow"), lax.axis_index("ccol"), lax.axis_index("lvl")
    rhs, width = 8, x_ref.shape[1]
    n_near, n_groups = near.shape[0], left.shape[0]
    n_far = n_groups * GROUP
    rank = width // GROUP
    near_step = n_near // near_sem.shape[0]
    rp, cp = n_col * n_lvl, n_row * n_lvl
    me_r, me_c = c * n_lvl + k, r * n_lvl + k

    nx = 4 if n_row % 4 == 0 else n_row
    ny = n_row // nx
    y, x = r // nx, lax.rem(r, nx)
    zs = [c] + [lax.rem(c + o, n_col) for o in range(1, n_col)]
    ys = [y] + [lax.rem(y + o, ny) for o in range(1, ny)]
    xs = [x] + [lax.rem(x + o, nx) for o in range(1, nx)]
    ks = [k] + [lax.rem(k + o, n_lvl) for o in range(1, n_lvl)]
    row_peers, col_peers, row_far, col_far = [], [], [], []
    for oz in far_first(n_col):
        for ok in range(n_lvl):
            if oz or ok:
                row_peers.append((zs[oz] * n_lvl + ks[ok], {"crow": r, "ccol": zs[oz], "lvl": ks[ok]}))
                row_far.append(min(oz, n_col - oz))
    grid = [(oy, ox) for oy in range(ny) for ox in range(nx)]
    grid.sort(key=lambda o: -min(o[0], ny - o[0]) - min(o[1], nx - o[1]))
    for oy, ox in grid:
        to = ys[oy] * nx + xs[ox]
        for ok in range(n_lvl):
            if oy or ox or ok:
                col_peers.append((to * n_lvl + ks[ok], {"crow": to, "ccol": c, "lvl": ks[ok]}))
                col_far.append(min(oy, ny - oy) + min(ox, nx - ox))

    barrier = pltpu.get_barrier_semaphore()
    other = {"lvl": 1 - k}
    for ahead, peers in ((0, col_peers), (1, row_peers)):
        for at in reversed(range(0, len(peers) - 1, n_lvl)):
            where = {**peers[at][1], "lvl": jnp.int32(ahead)}
            pl.semaphore_signal(barrier, inc=1, device_id=where, device_id_type=MESH)

        @pl.when(k != ahead)
        def _():
            pl.semaphore_signal(barrier, inc=1, device_id=other, device_id_type=MESH)

    small = [
        pltpu.make_async_copy(src, dst, small_sem.at[i])
        for i, (src, dst) in enumerate(
            ((x_hbm, x_ref), (np_hbm, np_v), (fp_hbm, fp_v), (cnt_hbm, cnt_s), (np_hbm, np_s), (fp_hbm, fp_s))
        )
    ]
    for copy in small:
        copy.start()
    far_copies = [
        pltpu.make_async_copy(left_hbm, left, far_sem.at[0]),
        pltpu.make_async_copy(right_hbm, right, far_sem.at[1]),
    ]

    def near_copy(step):
        part = pl.ds(step * near_step, near_step)
        return pltpu.make_async_copy(near_hbm.at[part], near.at[part], near_sem.at[step])

    for copy in far_copies:
        copy.start()
    for step in range(near_sem.shape[0]):
        near_copy(step).start()

    small[0].wait()
    def meet(ahead, peers):
        @pl.when(k == ahead)
        def _():
            pl.semaphore_wait(barrier, len(peers))
            pl.semaphore_signal(ready, inc=1, device_id=other, device_id_type=MESH)

        @pl.when(k != ahead)
        def _():
            pl.semaphore_wait(ready, 1)

    def give_x(where, buf, mine, sem):
        pltpu.make_async_remote_copy(
            src_ref=x_ref, dst_ref=buf.at[mine], send_sem=gsend, recv_sem=sem,
            device_id=where, device_id_type=MESH,
        ).start()

    def meet_cols():
        meet(0, col_peers)
        for _, where in col_peers:
            give_x(where, col_in, me_c, gcol)

    def meet_rows():
        meet(1, row_peers)
        for _, where in row_peers:
            give_x(where, row_in, me_r, grow)

    def meet_both():
        meet(0, col_peers)
        meet(1, row_peers)
        todo = [(far, where, col_in, me_c, gcol) for far, (_, where) in zip(col_far, col_peers)]
        todo += [(far, where, row_in, me_r, grow) for far, (_, where) in zip(row_far, row_peers)]
        for _, *args in sorted(todo, key=lambda item: -item[0]):
            give_x(*args)

    def rows_at(stage):
        for plane, at in enumerate(STAGES):
            if at == stage:
                pl.when(c == plane)(meet_rows)

    pl.when(c >= len(STAGES))(meet_both)
    pl.when(c < len(STAGES))(meet_cols)
    rows_at(0)
    row_in[me_r] = x_ref[...]
    col_in[me_c] = x_ref[...]
    for copy in small[1:]:
        copy.wait()
    tab_v[...] = jnp.zeros_like(tab_v)
    zero = jnp.zeros((rhs, width), F32)
    for total in (row_n, row_f, col_n, col_f):
        total[0] = zero
    for pairs, count, at in ((np_v, 0, 0), (fp_v, 1, 2)):
        slots = pairs.shape[1]
        for which in range(2):
            prev, last = chain_tables(pairs[...], cnt_s[count], which)
            tab_v[at + which : at + which + 1, :slots] = prev
            tab_v[4 + at + which : 5 + at + which, :slots] = last
    tab_copy = pltpu.make_async_copy(tab_v, tab_s, tab_sem)
    tab_copy.start()

    for copy in far_copies:
        copy.wait()

    def far_turn(g, carry):
        left_t[g] = left[g].T
        right_t[g] = right[g].T
        return carry

    lax.fori_loop(0, n_groups, far_turn, 0, unroll=4)
    rows_at(1)

    def near_turn(step, carry):
        near_copy(step).wait()
        for u in range(near_step):
            slot = step * near_step + u
            near_t[slot] = near[slot].T
        return carry

    steps = near_sem.shape[0]
    lax.fori_loop(0, steps // 2, near_turn, 0)
    rows_at(2)
    lax.fori_loop(steps // 2, 3 * steps // 4, near_turn, 0)
    rows_at(3)
    lax.fori_loop(3 * steps // 4, steps, near_turn, 0)
    tab_copy.wait()
    rows_at(4)

    def drain(buf, count, sem):
        part = buf.at[pl.ds(0, count)]
        pltpu.make_async_copy(part, part, sem).wait()

    def unpack(src, dst):
        def body(a, carry):
            for kk in range(n_lvl):
                v = src[a * n_lvl + kk].astype(F32).reshape(2, rhs, width)
                for jj in range(2):
                    dst[a * 2 * n_lvl + jj * n_lvl + kk] = v[jj]
            return carry

        lax.fori_loop(0, src.shape[0] // n_lvl, body, 0, unroll=8)

    diag = (
        lax.broadcasted_iota(jnp.int32, (GROUP * rhs, width), 0) // rhs
        == lax.broadcasted_iota(jnp.int32, (GROUP * rhs, width), 1) // rank
    )
    def one_way(field, side, blocks, first, second, near_sum, far_sum, chain):
        every = n_near // n_groups

        def coefficients(g):
            v = jnp.concatenate([field[fp_s[side, g * GROUP + w]] for w in range(GROUP)], 0)
            coef = jnp.dot(v.astype(BF16), first[g], preferred_element_type=F32)
            return jnp.where(diag, coef, 0.0).astype(BF16)

        def near_slot(slot):
            v = field[np_s[side, slot]].astype(BF16)
            part = jnp.dot(v, blocks[slot], preferred_element_type=F32)
            near_sum[slot + 1] = part + near_sum[tab_s[chain, slot]]

        def far_group(g, coef):
            part = jnp.dot(coef, second[g], preferred_element_type=F32)
            for w in range(GROUP):
                slot = g * GROUP + w
                far_sum[slot + 1] = part[w * rhs : (w + 1) * rhs] + far_sum[tab_s[2 + chain, slot]]

        coefs = {}
        for g in range(n_groups + LAG):
            if g < n_groups:
                coefs[g] = coefficients(g)
                for slot in range(g * every, (g + 1) * every):
                    near_slot(slot)
            if g >= LAG:
                far_group(g - LAG, coefs.pop(g - LAG))

    def collect(near_sum, far_sum, chain, out, to):
        first = 2 * n_lvl * (to // n_lvl) + lax.rem(to, n_lvl)
        parts = []
        for jj in range(2):
            p = first + jj * n_lvl
            parts.append(near_sum[tab_s[4 + chain, p]] + far_sum[tab_s[6 + chain, p]])
        out[to] = jnp.concatenate(parts, 0).astype(BF16)

    def give_back(src, dst, mine, sem, to, where):
        pltpu.make_async_remote_copy(
            src_ref=src.at[to], dst_ref=dst.at[mine], send_sem=rsend, recv_sem=sem,
            device_id=where, device_id_type=MESH,
        ).start()

    def give_all(near_sum, far_sum, chain, peers, src, dst, mine, sem):
        for at in range(0, len(peers), CHUNK):
            for to, _ in peers[at : at + CHUNK]:
                collect(near_sum, far_sum, chain, src, to)
            for peer in peers[at : at + CHUNK]:
                give_back(src, dst, mine, sem, *peer)
        collect(near_sum, far_sum, chain, dst, mine)

    drain(col_in, cp - 1, gcol)
    unpack(col_in, col_x)
    one_way(col_x, 1, near_t, right_t, left, row_n, row_f, 0)
    give_all(row_n, row_f, 0, row_peers, row_out, row_back, me_r, rrow)

    drain(row_in, rp - 1, grow)
    unpack(row_in, row_x)
    one_way(row_x, 0, near, left_t, right, col_n, col_f, 1)
    give_all(col_n, col_f, 1, col_peers, col_out, col_back, me_c, rcol)

    drain(row_back, rp - 1, rrow)
    total = row_back[0].astype(F32)
    for a in range(1, rp):
        total = total + row_back[a].astype(F32)
    drain(col_back, cp - 1, rcol)
    for a in range(cp):
        total = total + col_back[a].astype(F32)
    out_ref[...] = total
    drain(row_in, rp - 1, gsend)
    drain(col_in, cp - 1, gsend)
    drain(row_back, rp - 1, rsend)
    drain(col_back, cp - 1, rsend)


def per_device(x_field, near_blocks, near_pairs, far_left, far_right, far_pairs, tile_counts):
    n_row, n_col, n_lvl = (lax.axis_size(a) for a in ("crow", "ccol", "lvl"))
    per, rhs, width = x_field.shape[1], x_field.shape[3], x_field.shape[4]
    n_near, n_far, rank = near_blocks.shape[3], far_left.shape[3], far_left.shape[4]
    n_groups = n_far // GROUP
    x = x_field.reshape(per * rhs, width)
    near = near_blocks.reshape(n_near, width, width)
    left = far_left.reshape(n_groups, GROUP * rank, width)
    right = far_right.reshape(n_groups, GROUP * rank, width)
    npairs = near_pairs.reshape(n_near, 2).T
    fpairs = far_pairs.reshape(n_far, 2).T
    counts = tile_counts.reshape(2)
    rp, cp = n_col * n_lvl, n_row * n_lvl
    rows, cols = per * rp, per * cp
    vmem = pl.BlockSpec(memory_space=pltpu.VMEM)
    hbm = pl.BlockSpec(memory_space=pltpu.HBM)
    dma = pltpu.SemaphoreType.DMA
    operands = [
        pltpu.with_memory_space_constraint(a, pltpu.HBM)
        for a in (x, near, left, right, npairs, fpairs, counts)
    ]
    out = pl.pallas_call(
        functools.partial(kernel, n_row, n_col, n_lvl),
        out_shape=jax.ShapeDtypeStruct((per * rhs, width), F32),
        in_specs=[hbm] * 7,
        out_specs=vmem,
        scratch_shapes=[
            pltpu.VMEM(x.shape, BF16),
            pltpu.SMEM(npairs.shape, jnp.int32),
            pltpu.SMEM(fpairs.shape, jnp.int32),
            pltpu.SMEM(counts.shape, jnp.int32),
            pltpu.VMEM(npairs.shape, jnp.int32),
            pltpu.VMEM(fpairs.shape, jnp.int32),
            pltpu.VMEM((8, 128), jnp.int32),
            pltpu.SMEM((8, 128), jnp.int32),
            pltpu.VMEM(near.shape, BF16),
            pltpu.VMEM(left.shape, BF16),
            pltpu.VMEM(right.shape, BF16),
            pltpu.VMEM(near.shape, BF16),
            pltpu.VMEM(left.shape, BF16),
            pltpu.VMEM(right.shape, BF16),
            pltpu.VMEM((rp, per * rhs, width), BF16),
            pltpu.VMEM((cp, per * rhs, width), BF16),
            pltpu.VMEM((rows, rhs, width), F32),
            pltpu.VMEM((cols, rhs, width), F32),
            pltpu.VMEM((n_near + 1, rhs, width), F32),
            pltpu.VMEM((n_far + 1, rhs, width), F32),
            pltpu.VMEM((n_near + 1, rhs, width), F32),
            pltpu.VMEM((n_far + 1, rhs, width), F32),
            pltpu.VMEM((rp, per * rhs, width), BF16),
            pltpu.VMEM((cp, per * rhs, width), BF16),
            pltpu.VMEM((rp, per * rhs, width), BF16),
            pltpu.VMEM((cp, per * rhs, width), BF16),
            dma((6,)),
            dma((2,)),
            dma((8,)),
            dma, dma, dma, dma, dma, dma, dma,
            pltpu.SemaphoreType.REGULAR,
        ],
        compiler_params=pltpu.CompilerParams(
            collective_id=0, has_side_effects=True, vmem_limit_bytes=40 * 1024 * 1024
        ),
        cost_estimate=pl.CostEstimate(
            flops=4 * (n_near + n_far) * rhs * width * width,
            bytes_accessed=2 * (near.size + left.size + right.size),
            transcendentals=0,
        ),
    )(*operands)
    return out.reshape(x_field.shape)


def solution(mesh):
    placed = (
        P("crow", "ccol", "lvl", None, None),
        P("crow", "ccol", "lvl", None, None, None),
        P("crow", "ccol", "lvl", None, None),
        P("crow", "ccol", "lvl", None, None, None),
        P("crow", "ccol", "lvl", None, None, None),
        P("crow", "ccol", "lvl", None, None),
        P("crow", "ccol", "lvl", None),
    )
    return jax.shard_map(
        per_device,
        mesh=mesh,
        in_specs=placed,
        out_specs=P("crow", "ccol", "lvl", None, None),
        check_vma=False,
    )
```

```python
import functools

import jax
import jax.numpy as jnp
from jax import lax
from jax.experimental import pallas as pl
from jax.experimental.pallas import tpu as pltpu
from jax.sharding import PartitionSpec as P

TILE = 4
GROUP = 8
CHUNK = 8
LAG = 1
STAGES = (3, 2, 1, 0)
F32 = jnp.float32
BF16 = jnp.bfloat16
MESH = pl.DeviceIdType.MESH


def far_first(n):
    return sorted(range(n), key=lambda o: -min(o, n - o))


def chain_tables(pairs, count, which):
    slots = pairs.shape[1]
    by_lane = jnp.broadcast_to(pairs[which : which + 1, :], (slots, slots)).astype(F32)
    by_row = by_lane.T
    t = lax.broadcasted_iota(jnp.int32, (slots, slots), 0)
    s = lax.broadcasted_iota(jnp.int32, (slots, slots), 1)
    before = (by_row == by_lane) & (t < s)
    prev = jnp.max(jnp.where(before, t + 1, 0), axis=0, keepdims=True)
    mine = (by_row == s.astype(F32)) & (t < count * TILE)
    last = jnp.max(jnp.where(mine, t + 1, 0), axis=0, keepdims=True)
    return prev, last


def kernel(
    n_row, n_col, n_lvl,
    x_hbm, near_hbm, left_hbm, right_hbm, np_hbm, fp_hbm, cnt_hbm,
    out_ref,
    x_ref, np_s, fp_s, cnt_s, np_v, fp_v, tab_v, tab_s,
    near, left, right, near_t, left_t, right_t,
    row_in, col_in, row_x, col_x, row_n, row_f, col_n, col_f,
    row_out, col_out, row_back, col_back,
    small_sem, far_sem, near_sem, tab_sem, gsend, grow, gcol, rsend, rrow, rcol, ready,
):
    r, c, k = lax.axis_index("crow"), lax.axis_index("ccol"), lax.axis_index("lvl")
    rhs, width = 8, x_ref.shape[1]
    n_near, n_groups = near.shape[0], left.shape[0]
    n_far = n_groups * GROUP
    rank = width // GROUP
    near_step = n_near // near_sem.shape[0]
    rp, cp = n_col * n_lvl, n_row * n_lvl
    me_r, me_c = c * n_lvl + k, r * n_lvl + k

    nx = 4 if n_row % 4 == 0 else n_row
    ny = n_row // nx
    y, x = r // nx, lax.rem(r, nx)
    zs = [c] + [lax.rem(c + o, n_col) for o in range(1, n_col)]
    ys = [y] + [lax.rem(y + o, ny) for o in range(1, ny)]
    xs = [x] + [lax.rem(x + o, nx) for o in range(1, nx)]
    ks = [k] + [lax.rem(k + o, n_lvl) for o in range(1, n_lvl)]
    row_peers, col_peers, row_far, col_far = [], [], [], []
    for oz in far_first(n_col):
        for ok in range(n_lvl):
            if oz or ok:
                row_peers.append((zs[oz] * n_lvl + ks[ok], {"crow": r, "ccol": zs[oz], "lvl": ks[ok]}))
                row_far.append(min(oz, n_col - oz))
    grid = [(oy, ox) for oy in range(ny) for ox in range(nx)]
    grid.sort(key=lambda o: -min(o[0], ny - o[0]) - min(o[1], nx - o[1]))
    for oy, ox in grid:
        to = ys[oy] * nx + xs[ox]
        for ok in range(n_lvl):
            if oy or ox or ok:
                col_peers.append((to * n_lvl + ks[ok], {"crow": to, "ccol": c, "lvl": ks[ok]}))
                col_far.append(min(oy, ny - oy) + min(ox, nx - ox))

    barrier = pltpu.get_barrier_semaphore()
    other = {"lvl": 1 - k}
    for ahead, peers in ((0, col_peers), (1, row_peers)):
        for at in reversed(range(0, len(peers) - 1, n_lvl)):
            where = {**peers[at][1], "lvl": jnp.int32(ahead)}
            pl.semaphore_signal(barrier, inc=1, device_id=where, device_id_type=MESH)

        @pl.when(k != ahead)
        def _():
            pl.semaphore_signal(barrier, inc=1, device_id=other, device_id_type=MESH)

    small = [
        pltpu.make_async_copy(src, dst, small_sem.at[i])
        for i, (src, dst) in enumerate(
            ((x_hbm, x_ref), (np_hbm, np_v), (fp_hbm, fp_v), (cnt_hbm, cnt_s), (np_hbm, np_s), (fp_hbm, fp_s))
        )
    ]
    for copy in small:
        copy.start()
    far_copies = [
        pltpu.make_async_copy(left_hbm, left, far_sem.at[0]),
        pltpu.make_async_copy(right_hbm, right, far_sem.at[1]),
    ]

    def near_copy(step):
        part = pl.ds(step * near_step, near_step)
        return pltpu.make_async_copy(near_hbm.at[part], near.at[part], near_sem.at[step])

    for copy in far_copies:
        copy.start()
    for step in range(near_sem.shape[0]):
        near_copy(step).start()

    small[0].wait()
    def meet(ahead, peers):
        @pl.when(k == ahead)
        def _():
            pl.semaphore_wait(barrier, len(peers))
            pl.semaphore_signal(ready, inc=1, device_id=other, device_id_type=MESH)

        @pl.when(k != ahead)
        def _():
            pl.semaphore_wait(ready, 1)

    def give_x(where, buf, mine, sem):
        pltpu.make_async_remote_copy(
            src_ref=x_ref, dst_ref=buf.at[mine], send_sem=gsend, recv_sem=sem,
            device_id=where, device_id_type=MESH,
        ).start()

    def meet_cols():
        meet(0, col_peers)
        for _, where in col_peers:
            give_x(where, col_in, me_c, gcol)

    def meet_rows():
        meet(1, row_peers)
        for _, where in row_peers:
            give_x(where, row_in, me_r, grow)

    def meet_both():
        meet(0, col_peers)
        meet(1, row_peers)
        todo = [(far, where, col_in, me_c, gcol) for far, (_, where) in zip(col_far, col_peers)]
        todo += [(far, where, row_in, me_r, grow) for far, (_, where) in zip(row_far, row_peers)]
        for _, *args in sorted(todo, key=lambda item: -item[0]):
            give_x(*args)

    def rows_at(stage):
        for plane, at in enumerate(STAGES):
            if at == stage:
                pl.when(c == plane)(meet_rows)

    pl.when(c >= len(STAGES))(meet_both)
    pl.when(c < len(STAGES))(meet_cols)
    rows_at(0)
    row_in[me_r] = x_ref[...]
    col_in[me_c] = x_ref[...]
    for copy in small[1:]:
        copy.wait()
    tab_v[...] = jnp.zeros_like(tab_v)
    zero = jnp.zeros((rhs, width), F32)
    for total in (row_n, row_f, col_n, col_f):
        total[0] = zero
    for pairs, count, at in ((np_v, 0, 0), (fp_v, 1, 2)):
        slots = pairs.shape[1]
        for which in range(2):
            prev, last = chain_tables(pairs[...], cnt_s[count], which)
            tab_v[at + which : at + which + 1, :slots] = prev
            tab_v[4 + at + which : 5 + at + which, :slots] = last
    tab_copy = pltpu.make_async_copy(tab_v, tab_s, tab_sem)
    tab_copy.start()

    for copy in far_copies:
        copy.wait()

    def far_turn(g, carry):
        left_t[g] = left[g].T
        right_t[g] = right[g].T
        return carry

    lax.fori_loop(0, n_groups, far_turn, 0, unroll=4)
    rows_at(1)

    def near_turn(step, carry):
        near_copy(step).wait()
        for u in range(near_step):
            slot = step * near_step + u
            near_t[slot] = near[slot].T
        return carry

    steps = near_sem.shape[0]
    lax.fori_loop(0, steps // 2, near_turn, 0)
    rows_at(2)
    lax.fori_loop(steps // 2, 3 * steps // 4, near_turn, 0)
    rows_at(3)
    lax.fori_loop(3 * steps // 4, steps, near_turn, 0)
    tab_copy.wait()
    rows_at(4)

    def drain(buf, count, sem):
        part = buf.at[pl.ds(0, count)]
        pltpu.make_async_copy(part, part, sem).wait()

    def unpack(src, dst):
        def body(a, carry):
            for kk in range(n_lvl):
                v = src[a * n_lvl + kk].astype(F32).reshape(2, rhs, width)
                for jj in range(2):
                    dst[a * 2 * n_lvl + jj * n_lvl + kk] = v[jj]
            return carry

        lax.fori_loop(0, src.shape[0] // n_lvl, body, 0, unroll=8)

    diag = (
        lax.broadcasted_iota(jnp.int32, (GROUP * rhs, width), 0) // rhs
        == lax.broadcasted_iota(jnp.int32, (GROUP * rhs, width), 1) // rank
    )
    def one_way(field, side, blocks, first, second, near_sum, far_sum, chain):
        every = n_near // n_groups

        def coefficients(g):
            v = jnp.concatenate([field[fp_s[side, g * GROUP + w]] for w in range(GROUP)], 0)
            coef = jnp.dot(v.astype(BF16), first[g], preferred_element_type=F32)
            return jnp.where(diag, coef, 0.0).astype(BF16)

        def near_slot(slot):
            v = field[np_s[side, slot]].astype(BF16)
            part = jnp.dot(v, blocks[slot], preferred_element_type=F32)
            near_sum[slot + 1] = part + near_sum[tab_s[chain, slot]]

        def far_group(g, coef):
            part = jnp.dot(coef, second[g], preferred_element_type=F32)
            for w in range(GROUP):
                slot = g * GROUP + w
                far_sum[slot + 1] = part[w * rhs : (w + 1) * rhs] + far_sum[tab_s[2 + chain, slot]]

        coefs = {}
        for g in range(n_groups + LAG):
            if g < n_groups:
                coefs[g] = coefficients(g)
                for slot in range(g * every, (g + 1) * every):
                    near_slot(slot)
            if g >= LAG:
                far_group(g - LAG, coefs.pop(g - LAG))

    def collect(near_sum, far_sum, chain, out, to):
        first = 2 * n_lvl * (to // n_lvl) + lax.rem(to, n_lvl)
        parts = []
        for jj in range(2):
            p = first + jj * n_lvl
            parts.append(near_sum[tab_s[4 + chain, p]] + far_sum[tab_s[6 + chain, p]])
        out[to] = jnp.concatenate(parts, 0).astype(BF16)

    def give_back(src, dst, mine, sem, to, where):
        pltpu.make_async_remote_copy(
            src_ref=src.at[to], dst_ref=dst.at[mine], send_sem=rsend, recv_sem=sem,
            device_id=where, device_id_type=MESH,
        ).start()

    def give_all(near_sum, far_sum, chain, peers, src, dst, mine, sem):
        for at in range(0, len(peers), CHUNK):
            for to, _ in peers[at : at + CHUNK]:
                collect(near_sum, far_sum, chain, src, to)
            for peer in peers[at : at + CHUNK]:
                give_back(src, dst, mine, sem, *peer)
        collect(near_sum, far_sum, chain, dst, mine)

    drain(col_in, cp - 1, gcol)
    unpack(col_in, col_x)
    one_way(col_x, 1, near_t, right_t, left, row_n, row_f, 0)
    give_all(row_n, row_f, 0, row_peers, row_out, row_back, me_r, rrow)

    drain(row_in, rp - 1, grow)
    unpack(row_in, row_x)
    one_way(row_x, 0, near, left_t, right, col_n, col_f, 1)
    give_all(col_n, col_f, 1, col_peers, col_out, col_back, me_c, rcol)

    def added(parts):
        while len(parts) > 1:
            odd = parts[-1:] if len(parts) % 2 else []
            parts = [p + q for p, q in zip(parts[::2], parts[1::2])] + odd
        return parts[0]

    drain(row_in, rp - 1, gsend)
    drain(col_in, cp - 1, gsend)
    drain(row_back, rp - 1, rrow)
    total = added([row_back[a].astype(F32) for a in range(rp)])
    drain(col_back, cp - 1, rcol)
    out_ref[...] = total + added([col_back[a].astype(F32) for a in range(cp)])
    drain(row_back, rp - 1, rsend)
    drain(col_back, cp - 1, rsend)


def per_device(x_field, near_blocks, near_pairs, far_left, far_right, far_pairs, tile_counts):
    n_row, n_col, n_lvl = (lax.axis_size(a) for a in ("crow", "ccol", "lvl"))
    per, rhs, width = x_field.shape[1], x_field.shape[3], x_field.shape[4]
    n_near, n_far, rank = near_blocks.shape[3], far_left.shape[3], far_left.shape[4]
    n_groups = n_far // GROUP
    x = x_field.reshape(per * rhs, width)
    near = near_blocks.reshape(n_near, width, width)
    left = far_left.reshape(n_groups, GROUP * rank, width)
    right = far_right.reshape(n_groups, GROUP * rank, width)
    npairs = near_pairs.reshape(n_near, 2).T
    fpairs = far_pairs.reshape(n_far, 2).T
    counts = tile_counts.reshape(2)
    rp, cp = n_col * n_lvl, n_row * n_lvl
    rows, cols = per * rp, per * cp
    vmem = pl.BlockSpec(memory_space=pltpu.VMEM)
    hbm = pl.BlockSpec(memory_space=pltpu.HBM)
    dma = pltpu.SemaphoreType.DMA
    operands = [
        pltpu.with_memory_space_constraint(a, pltpu.HBM)
        for a in (x, near, left, right, npairs, fpairs, counts)
    ]
    out = pl.pallas_call(
        functools.partial(kernel, n_row, n_col, n_lvl),
        out_shape=jax.ShapeDtypeStruct((per * rhs, width), F32),
        in_specs=[hbm] * 7,
        out_specs=vmem,
        scratch_shapes=[
            pltpu.VMEM(x.shape, BF16),
            pltpu.SMEM(npairs.shape, jnp.int32),
            pltpu.SMEM(fpairs.shape, jnp.int32),
            pltpu.SMEM(counts.shape, jnp.int32),
            pltpu.VMEM(npairs.shape, jnp.int32),
            pltpu.VMEM(fpairs.shape, jnp.int32),
            pltpu.VMEM((8, 128), jnp.int32),
            pltpu.SMEM((8, 128), jnp.int32),
            pltpu.VMEM(near.shape, BF16),
            pltpu.VMEM(left.shape, BF16),
            pltpu.VMEM(right.shape, BF16),
            pltpu.VMEM(near.shape, BF16),
            pltpu.VMEM(left.shape, BF16),
            pltpu.VMEM(right.shape, BF16),
            pltpu.VMEM((rp, per * rhs, width), BF16),
            pltpu.VMEM((cp, per * rhs, width), BF16),
            pltpu.VMEM((rows, rhs, width), F32),
            pltpu.VMEM((cols, rhs, width), F32),
            pltpu.VMEM((n_near + 1, rhs, width), F32),
            pltpu.VMEM((n_far + 1, rhs, width), F32),
            pltpu.VMEM((n_near + 1, rhs, width), F32),
            pltpu.VMEM((n_far + 1, rhs, width), F32),
            pltpu.VMEM((rp, per * rhs, width), BF16),
            pltpu.VMEM((cp, per * rhs, width), BF16),
            pltpu.VMEM((rp, per * rhs, width), BF16),
            pltpu.VMEM((cp, per * rhs, width), BF16),
            dma((6,)),
            dma((2,)),
            dma((8,)),
            dma, dma, dma, dma, dma, dma, dma,
            pltpu.SemaphoreType.REGULAR,
        ],
        compiler_params=pltpu.CompilerParams(
            collective_id=0, has_side_effects=True, vmem_limit_bytes=40 * 1024 * 1024
        ),
        cost_estimate=pl.CostEstimate(
            flops=4 * (n_near + n_far) * rhs * width * width,
            bytes_accessed=2 * (near.size + left.size + right.size),
            transcendentals=0,
        ),
    )(*operands)
    return out.reshape(x_field.shape)


def solution(mesh):
    placed = (
        P("crow", "ccol", "lvl", None, None),
        P("crow", "ccol", "lvl", None, None, None),
        P("crow", "ccol", "lvl", None, None),
        P("crow", "ccol", "lvl", None, None, None),
        P("crow", "ccol", "lvl", None, None, None),
        P("crow", "ccol", "lvl", None, None),
        P("crow", "ccol", "lvl", None),
    )
    return jax.shard_map(
        per_device,
        mesh=mesh,
        in_specs=placed,
        out_specs=P("crow", "ccol", "lvl", None, None),
        check_vma=False,
    )
```
